256 devices in a mesh: tile: 32 (over y, z_hi, core), trc: 8 (over x, z_lo).
Axes of the slice: x: 4, y: 4, z: 8 (z_hi: 4, z_lo: 2; z = z_hi * 2 + z_lo), core: 2. Of those that a mesh axis runs over, the one named last changes fastest.
Arguments:
- tracers: float32 [64, 48, 256, 256], P('trc', None, 'tile'), may hold values from -6 to 6
- archive: bfloat16 [8, 4, 48, 256, 256], P('trc', None, None, 'tile'), may hold values from -0.14941406 to 0.14941406
- sea_mask: int32 [256, 256], P('tile'), may hold values 0 or 1
- levels: int32 [256, 256], P('tile'), may hold values from 1 to 48
Outputs:
- transported: float32 [64, 48, 256, 256], P('trc', None, 'tile')
The draws below stay inside these ranges and needn't reach their ends.
All inputs are finite; a program needn't handle non-finite values. No bound on the sum of `sea_mask` on one device may be relied on, other than what follows from the above.
Results may differ from the reference program's by a relative error of at most 0.00055.
Values may be sent and summed in bfloat16 or wider, within the bound.
A program may use at most 64 MiB of HBM per device.

```python
import jax
import jax.numpy as jnp
from jax import lax

LEV = 48
CY = 256
STEPS = 3
NX = 256
NTRC = 64
N_TRC = 8


def set_ends(result, rng, smallest, top_value):
    longest = result.shape.index(max(result.shape))
    spots = []
    for shift in (0, 1):
        where = [jax.random.randint(jax.random.fold_in(rng, axis), (), 0, length) for axis, length in enumerate(result.shape)]
        where[longest] = (where[longest] + shift) % result.shape[longest]
        spots.append(tuple(where))
    return result.at[spots[0]].set(smallest).at[spots[1]].set(top_value)


def block_scale(stream_key, dims, pieces, least, largest):
    def one(axis_at, parts):
        heights = jax.random.uniform(jax.random.fold_in(jax.random.fold_in(stream_key, 6), axis_at), (parts,), jnp.float32, least / len(pieces), largest / len(pieces))
        return jnp.repeat(jnp.exp(heights), dims[axis_at] // parts).reshape((-1,) + (1,) * (len(dims) - axis_at - 1))

    loudness = one(*pieces[0])
    for cut in pieces[1:]:
        loudness = loudness * one(*cut)
    return loudness


def noise(stream_key, dims, deviation, limit, shards=(), kind=jnp.bfloat16):
    gain = block_scale(stream_key, dims, shards, -0.22, 0.18) if shards else 1.0
    entries = jax.random.normal(stream_key, dims, jnp.float32) * deviation * gain
    return jnp.minimum(jnp.maximum(entries, -limit), limit).astype(kind)


def setup_inputs(seed: int = 0) -> dict:
    key_of = jax.random.split(jax.random.key(seed), 5)
    tracers = noise(key_of[0], (NTRC, LEV, NX, CY), 1.0, 6.0, ((0, 8), (2, 32)), jnp.float32)
    archive = jnp.clip(jax.random.uniform(key_of[1], (N_TRC, 4, LEV, NX, CY), jnp.float32, -0.14941406, 0.14941406) * block_scale(key_of[1], (N_TRC, 4, LEV, NX, CY), ((0, 8), (3, 32)), -0.4, 0.0), -0.14941406, 0.14941406).astype(jnp.bfloat16)
    sea_mask = set_ends((jax.random.randint(key_of[2], (NX, CY), 0, 4) < 3).astype(jnp.int32), jax.random.fold_in(key_of[2], 1), 0, 1)
    levels = set_ends(jax.random.randint(key_of[3], (NX, CY), 1, LEV + 1), jax.random.fold_in(key_of[3], 1), 1, LEV).astype(jnp.int32)
    return dict(tracers=tracers, archive=archive, sea_mask=sea_mask, levels=levels)


DIFFUSION = 0.04
MIX_SCALE = 0.3


def face_flux(left_vals, right_vals, left_wet, right_wet, courant):
    moved = jnp.maximum(courant, 0.0) * left_vals + jnp.minimum(courant, 0.0) * right_vals
    return (moved + DIFFUSION * (left_vals - right_vals)) * (left_wet * right_wet)


def inner_change(tracer, wetness, fields):
    merid = fields[1][:, :, 1:]
    south = tracer[..., :-1]
    north = tracer[..., 1:]
    northward = face_flux(south, north, wetness[:, :, :-1], wetness[:, :, 1:], merid)
    edge = jnp.zeros_like(northward[..., :1])
    padded = jnp.concatenate([edge, northward, edge], axis=-1)
    merid_change = padded[..., :-1] - padded[..., 1:]
    upward = fields[2][1:]
    mixing = MIX_SCALE * jnp.abs(fields[3][1:])
    above = tracer[..., :-1, :, :]
    below = tracer[..., 1:, :, :]
    moved = jnp.maximum(upward, 0.0) * below + jnp.minimum(upward, 0.0) * above
    rising = (moved + mixing * (below - above)) * (wetness[:-1] * wetness[1:])
    edge_v = jnp.zeros_like(rising[..., :1, :, :])
    padded_v = jnp.concatenate([edge_v, rising, edge_v], axis=-3)
    vert_change = padded_v[..., 1:, :, :] - padded_v[..., :-1, :, :]
    return merid_change, vert_change


def make_wetness(sea_mask, levels, depth):
    level_ids = jnp.arange(depth, dtype=jnp.int32)[:, None, None]
    return (sea_mask[None] * (level_ids < levels[None]).astype(jnp.int32)).astype(jnp.float32)


def advance(tracer, wetness, fields):
    zonal = fields[0]
    west_vals = jnp.roll(tracer, 1, axis=-2)
    west_wet = jnp.roll(wetness, 1, axis=-2)
    eastward = face_flux(west_vals, tracer, west_wet, wetness, zonal)
    zonal_change = eastward - jnp.roll(eastward, -1, axis=-2)
    merid_change, vert_change = inner_change(tracer, wetness, fields)
    return tracer + zonal_change + merid_change + vert_change


def reference(tracers, archive, sea_mask, levels):
    wetness = make_wetness(sea_mask, levels, LEV)
    current = tracers
    for turn_index in range(STEPS):
        fields = archive[turn_index % N_TRC].astype(jnp.float32)
        current = lax.map(lambda single: advance(single, wetness, fields), current)
    return current
```

```python
import functools

import jax
import jax.numpy as jnp
from jax import lax
from jax.experimental import pallas as pl
from jax.experimental.pallas import tpu as pltpu
from jax.sharding import PartitionSpec as P

MESH = pl.DeviceIdType.MESH
STEPS = 3
DIFFUSION = 0.04
MIX_SCALE = 0.3
TRACERS, LEV, LON, LAT = 8, 48, 8, 256
ROWS = LEV * LON
PAIRS = LEV // 2
TILES, GROUP = 32, 8

EVENTS = (
    (3, 99, 195, 96, 197, 100, 6, 98),
    (14, 107, 207, 201, 201, 195, 10, 104),
    (17, 113, 230, 105, 0, 201, 192, 122),
    (192, 122, 0, 113, 213, 108, 30, 3),
    (26, 11, 211, 225, 10, 122, 200, 8),
    (41, 130, 17, 9, 17, 117, 38, 134),
    (200, 139, 41, 137, 26, 211, 208, 192),
    (34, 147, 235, 194, 45, 0, 50, 26),
    (51, 155, 52, 145, 98, 8, 20, 136),
    (208, 1, 217, 50, 34, 130, 56, 201),
    (59, 192, 250, 124, 217, 43, 40, 148),
    (226, 162, 61, 152, 48, 140, 86, 35),
    (65, 177, 258, 210, 107, 26, 131, 112),
    (232, 200, 8, 0, 56, 144, 221, 154),
    (73, 170, 65, 59, 69, 34, 90, 208),
    (82, 187, 266, 128, 114, 225, 105, 17),
    (254, 50, 24, 181, 82, 156, 226, 166),
    (91, 251, 77, 75, 73, 56, 145, 41),
    (258, 32, 275, 26, 88, 67, 64, 174),
    (266, 208, 32, 188, 237, 162, 250, 83),
    (276, 17, 92, 40, 137, 177, 72, 50),
    (129, 58, 282, 248, 128, 170, 262, 225),
    (286, 275, 98, 91, 120, 73, 162, 217),
    (216, 40, 123, 32, 224, 234, 232, 186),
    (98, 24, 104, 17, 245, 48, 270, 65),
    (104, 81, 241, 64, 154, 89, 137, 56),
    (122, 72, 80, 272, 248, 80, 96, 176),
    (145, 281, 128, 160, 273, 16, 171, 259),
    (176, 224, 179, 80, 162, 243, 241, 250),
    (114, 88, 114, 168, 177, 184, 120, 72),
    (137, 64, 187, 281, 256, 248, 272, 274),
    (184, 217, 145, 234, 185, 256, 282, 267),
    (168, 257, 154, 240, 170, 281, 176, 88),
    (154, 265, 162, 217, 144, 264, 112, 241),
    (240, 234, 136, 256, 264, 272, 184, 280),
    (160, 240, 168, 264, 280, 216, 152, 232),
)
READY = ((14, 28, 24, 26, 31, 33), (27, 34, 35, 36, 36, 35), (14, 36, 36, 36, 36, 36))
SLABS = 6
AHEAD = 1
PIECES = SLABS * 2
SLAB_ROWS = ROWS // SLABS
SLAB_PAIRS = PAIRS // SLABS
EARLY = 6
VMEM_LIMIT = 48 * 2**20


def batch(j):
    low = 0 if j == 0 else SLAB_PAIRS * j - 1
    high = PAIRS if j == SLABS - 1 else SLAB_PAIRS * (j + 1) - 1
    return low, high


def by_rank(rank, values):
    total = jnp.int32(values[0])
    for r in range(1, GROUP):
        if values[r] != values[0]:
            total = jnp.where(rank == r, jnp.int32(values[r]), total)
    return total


def kernel(
    tracers, archive, sea_mask_hbm, levels_hbm, out,
    cur_a, cur_b, rec, rim_out, rim_in, halo, edge, masks, zonal_own, zrim_out, zrim_in, zrim, wet_out, wet_in, sea_mask, levels,
    load_sem, piece_send, piece_recv, rim_send, rim_recv, zrim_send, zrim_recv, wet_send, wet_recv, store_sem,
):
    tile = lax.axis_index("tile")
    rank = lax.axis_index("trc")
    x, z = rank // 2, rank % 2
    beside = (
        lax.rem(x + 1, 4) * 2 + z,
        lax.rem(x + 3, 4) * 2 + z,
        x * 2 + 1 - z,
    )
    east, west = lax.rem(tile + 1, TILES), lax.rem(tile + TILES - 1, TILES)

    first = pltpu.make_async_copy(tracers, cur_a.at[:, pl.ds(8, ROWS)], load_sem.at[0])
    own = pltpu.make_async_copy(archive.at[0], zonal_own, load_sem.at[1])

    def piece_ref(ref, record, half, slab):
        rows = pl.ds(pl.multiple_of(slab * SLAB_ROWS, SLAB_ROWS), SLAB_ROWS)
        if record is None:
            return ref.at[pl.ds(2 * half, 2), rows]
        return ref.at[record, pl.ds(2 * half, 2), rows]

    for r in range(STEPS):
        @pl.when(rank == r)
        def _():
            for j in range(SLABS):
                for h in range(2):
                    pltpu.make_async_copy(
                        piece_ref(archive, None, h, j), piece_ref(rec, r, h, j), piece_recv.at[r * PIECES + 2 * j + h]
                    ).start()

    own.start()
    maps = [
        pltpu.make_async_copy(src, dst, load_sem.at[2 + i])
        for i, (src, dst) in enumerate(((sea_mask_hbm, sea_mask), (levels_hbm, levels)))
    ]
    for c in maps:
        c.start()
    first.start()

    barrier = pltpu.get_barrier_semaphore()
    for k in range(1, GROUP):
        pl.semaphore_signal(barrier, inc=1, device_id={"trc": lax.rem(rank + k, GROUP)}, device_id_type=MESH)
    for n in (east, west):
        pl.semaphore_signal(barrier, inc=1, device_id={"tile": n}, device_id_type=MESH)

    row = lax.broadcasted_iota(jnp.int32, (2, LON, LAT), 1)
    lane = lax.broadcasted_iota(jnp.int32, (LON, LAT), 1)
    level_of = lax.broadcasted_iota(jnp.int32, (3, LON, LAT), 0)
    row_a = row[0]

    for c in maps:
        c.wait()
    depth = sea_mask[...] * levels[...]
    wet_out[...] = depth.astype(jnp.float32)
    for ref in (cur_a, cur_b):
        for t in range(TRACERS):
            ref[t, pl.ds(0, 8)] = jnp.zeros((8, LAT), jnp.float32)
            ref[t, pl.ds(ROWS + 8, 8)] = jnp.zeros((8, LAT), jnp.float32)
    pl.semaphore_wait(barrier, GROUP + 1)

    def tile_copy(src, dst, send, recv, to):
        return pltpu.make_async_remote_copy(
            src_ref=src, dst_ref=dst, send_sem=send, recv_sem=recv, device_id={"tile": to}, device_id_type=MESH
        )

    wet_copies = [
        tile_copy(wet_out, wet_in.at[side], wet_send.at[side], wet_recv.at[side], to)
        for side, to in ((0, east), (1, west))
    ]
    for c in wet_copies:
        c.start()

    words = []
    for e in range(0, len(EVENTS), 3):
        words.append(
            by_rank(rank, [sum(EVENTS[e + i][r] << (9 * i) for i in range(3)) for r in range(GROUP)])
        )

    def event_parts(e):
        code = (words[e // 3] // (1 << (9 * (e % 3)))) % 512
        return code // 8, code % 8

    def hand_on(p, d):
        ref = piece_ref(rec, p // PIECES, p % 2, (p % PIECES) // 2)
        return pltpu.make_async_remote_copy(
            src_ref=ref, dst_ref=ref, send_sem=piece_send.at[p, d], recv_sem=piece_recv.at[p],
            device_id={"trc": beside[d]}, device_id_type=MESH,
        )

    def event(e):
        p, dirs = event_parts(e)
        ref = piece_ref(rec, p // PIECES, p % 2, (p % PIECES) // 2)
        pltpu.make_async_copy(ref, ref, piece_recv.at[p]).wait()
        for d in range(3):
            if any((v >> d) & 1 for v in EVENTS[e]):
                @pl.when((dirs // (1 << d)) % 2 == 1)
                def _():
                    hand_on(p, d).start()

    def rim_copies(s, j):
        low, high = batch(j)
        rows = pl.ds(16 * low, 16 * (high - low))
        return [
            tile_copy(
                rim_out.at[s, side, rows], rim_in.at[s, side, rows], rim_send.at[s, side, j], rim_recv.at[s, side, j], to
            )
            for side, to in ((0, east), (1, west))
        ]

    def put_edges(t, value):
        for k in range(2):
            edge[0, pl.ds(2 * t + k, 1)] = value[k, 7:8]
            edge[1, pl.ds(2 * t + k, 1)] = value[k, 0:1]

    def put_rims(s, start):
        for side in range(2):
            rim_out[s, side, pl.ds(start, 16)] = edge[side].astype(jnp.bfloat16)

    def early_events():
        for e in range(EARLY):
            event(e)

    @pl.when(rank == 0)
    def _():
        early_events()

    def zrim_west(r):
        return tile_copy(zrim_out, zrim_in.at[r], zrim_send.at[0], zrim_recv.at[r], west)

    def zrim_round(r, k):
        return pltpu.make_async_remote_copy(
            src_ref=zrim_in.at[r], dst_ref=zrim_in.at[r], send_sem=zrim_send.at[k], recv_sem=zrim_recv.at[r],
            device_id={"trc": lax.rem(rank + k, GROUP)}, device_id_type=MESH,
        )

    own.wait()
    for g in range(LEV // 16):
        for q in range(8):
            value = zonal_own[pl.ds(128 * g + 16 * q, 16)].astype(jnp.float32).reshape(2, LON, LAT)
            for k in range(2):
                edge[0, pl.ds(2 * q + k, 1)] = value[k, 0:1]
        zrim_out[pl.ds(16 * g, 16)] = edge[0].astype(jnp.bfloat16)
    for r in range(STEPS):
        @pl.when(rank == r)
        def _():
            zrim_west(r).start()

    first.wait()
    for j in range(SLABS):
        low, high = batch(j)

        def first_rims(p, _):
            start = pl.multiple_of(16 * p, 16)
            for t in range(TRACERS):
                put_edges(t, cur_a[t, pl.ds(start + 8, 16)].reshape(2, LON, LAT))
            put_rims(0, start)
            return 0

        lax.fori_loop(low, high, first_rims, 0)
        for c in rim_copies(0, j):
            c.start()

    @pl.when(rank != 0)
    def _():
        early_events()

    for r in range(STEPS):
        @pl.when(rank == r)
        def _():
            zrim_west(r).wait_recv()
            for k in range(1, GROUP):
                zrim_round(r, k).start()

    for c in wet_copies:
        c.wait()
    depth_w, depth_e = wet_in[0, 7:8], wet_in[1, 0:1]
    depth_f = depth.astype(jnp.float32)
    beyond_w = jnp.where(row_a == 0, depth_w, pltpu.roll(depth_f, 1, 0))
    beyond_e = jnp.where(row_a == LON - 1, depth_e, pltpu.roll(depth_f, LON - 1, 0))
    beyond_s = jnp.where(lane == 0, 0.0, pltpu.roll(depth_f, 1, 1))
    beyond_n = jnp.where(lane == LAT - 1, 0.0, pltpu.roll(depth_f, LAT - 1, 1))
    for i, beyond in enumerate((beyond_w, beyond_e, beyond_s, beyond_n)):
        masks[i] = jnp.minimum(depth_f, beyond)
    masks[4] = depth_f

    def work(s, j, source, target):
        low, high = batch(j)
        for c in rim_copies(s, j):
            c.wait_recv()

        def pair(p, _):
            start = pl.multiple_of(16 * p, 16)
            after = pl.multiple_of(16 * p + 16, 16)
            level3 = (level_of + 2 * p).astype(jnp.float32)
            level2 = level3[:2]

            def field(f, at):
                return rec[s, f, pl.ds(at, 16)].astype(jnp.float32).reshape(2, LON, LAT)

            def two_sided(courant, mask):
                plus = jnp.maximum(courant, 0.0) + DIFFUSION
                wet = mask[None] > level2
                return jnp.where(wet, plus, 0.0), jnp.where(wet, plus - courant, 0.0)

            zonal = field(0, start)
            zonal_e = pltpu.roll(zonal, LON - 1, 1)
            rims = [jnp.broadcast_to(zrim[pl.ds(2 * p + k, 1)], (LON, LAT)) for k in range(2)]
            zonal_e = jnp.where(row == LON - 1, jnp.stack(rims), zonal_e)
            from_w, to_w = two_sided(zonal, masks[0])
            to_e, from_e = two_sided(zonal_e, masks[1])
            merid = field(1, start)
            from_s, to_s = two_sided(merid, masks[2])
            to_n, from_n = two_sided(pltpu.roll(merid, LAT - 1, 2), masks[3])
            upward = jnp.concatenate([field(2, start), field(2, after)[:1]], axis=0)
            mixing = MIX_SCALE * jnp.abs(jnp.concatenate([field(3, start), field(3, after)[:1]], axis=0))
            wet3 = jnp.logical_and(masks[4][None] > level3, level3 > 0.0)
            plus3 = jnp.maximum(upward, 0.0) + mixing
            lower = jnp.where(wet3, plus3, 0.0)
            upper = jnp.where(wet3, plus3 - upward, 0.0)
            from_below, to_above = lower[1:], lower[:2]
            from_above, to_below = upper[:2], upper[1:]
            stay = 1.0 - (to_w + to_e + to_s + to_n + to_above + to_below)

            for side in range(2):
                halo[side] = rim_in[s, side, pl.ds(start, 16)].astype(jnp.float32)
            for t in range(TRACERS):
                four = source[t, pl.ds(start, 32)].reshape(4, LON, LAT)
                here = four[1:3]
                side_w = jnp.stack([jnp.broadcast_to(halo[0, pl.ds(2 * t + k, 1)], (LON, LAT)) for k in range(2)])
                side_e = jnp.stack([jnp.broadcast_to(halo[1, pl.ds(2 * t + k, 1)], (LON, LAT)) for k in range(2)])
                at_w = jnp.where(row == 0, side_w, pltpu.roll(here, 1, 1))
                at_e = jnp.where(row == LON - 1, side_e, pltpu.roll(here, LON - 1, 1))
                new = stay * here + from_w * at_w + from_e * at_e
                new += from_s * pltpu.roll(here, 1, 2) + from_n * pltpu.roll(here, LAT - 1, 2)
                new += from_below * four[2:4] + from_above * four[0:2]
                target[t, pl.ds(pl.multiple_of(start + 8, 8), 16)] = new.reshape(16, LAT)
                if s < STEPS - 1:
                    put_edges(t, new)
            if s < STEPS - 1:
                put_rims(s + 1, start)
            return 0

        lax.fori_loop(low, high, pair, 0)
        if s < STEPS - 1:
            for c in rim_copies(s + 1, j):
                c.start()

    done = EARLY
    stores = []
    for s in range(STEPS):
        source, target = ((cur_a, cur_b), (cur_b, cur_a))[s % 2]
        for j in range(SLABS):
            upto = READY[s][j]
            if s < STEPS - 1 or j < SLABS - 1:
                upto = min(len(EVENTS), upto + AHEAD)
            for e in range(done, upto):
                event(e)
            done = max(done, upto)
            if j == 0:
                @pl.when(rank != s)
                def _():
                    zrim_west(s).wait_recv()
                zrim[...] = zrim_in[s].astype(jnp.float32)
            work(s, j, source, target)
            if s == STEPS - 1:
                low, high = batch(j)
                count = 16 * (high - low)
                c = pltpu.make_async_copy(
                    target.at[:, pl.ds(8 + 16 * low, count)], out.at[:, pl.ds(16 * low, count)], store_sem.at[j]
                )
                c.start()
                stores.append(c)

    for s in range(STEPS):
        for j in range(SLABS):
            for c in rim_copies(s, j):
                c.wait_send()
    for r in range(STEPS):
        @pl.when(rank == r)
        def _():
            zrim_west(r).wait_send()
            for k in range(1, GROUP):
                zrim_round(r, k).wait_send()
    for e in range(len(EVENTS)):
        p, dirs = event_parts(e)
        for d in range(3):
            if any((v >> d) & 1 for v in EVENTS[e]):
                @pl.when((dirs // (1 << d)) % 2 == 1)
                def _():
                    hand_on(p, d).wait_send()
    for c in stores:
        c.wait()


def per_device(tracers, archive, sea_mask, levels):
    any_space = pl.BlockSpec(memory_space=pl.ANY)
    in_hbm = pl.BlockSpec(memory_space=pltpu.HBM)
    dma = pltpu.SemaphoreType.DMA
    result = pl.pallas_call(
        kernel,
        out_shape=jax.ShapeDtypeStruct((TRACERS, ROWS, LAT), jnp.float32),
        in_specs=[in_hbm, in_hbm, in_hbm, in_hbm],
        out_specs=any_space,
        scratch_shapes=[
            pltpu.VMEM((TRACERS, ROWS + 16, LAT), jnp.float32),
            pltpu.VMEM((TRACERS, ROWS + 16, LAT), jnp.float32),
            pltpu.VMEM((STEPS, 4, ROWS + 16, LAT), jnp.bfloat16),
            pltpu.VMEM((STEPS, 2, ROWS, LAT), jnp.bfloat16),
            pltpu.VMEM((STEPS, 2, ROWS, LAT), jnp.bfloat16),
            pltpu.VMEM((2, 16, LAT), jnp.float32),
            pltpu.VMEM((2, 16, LAT), jnp.float32),
            pltpu.VMEM((5, LON, LAT), jnp.float32),
            pltpu.VMEM((ROWS, LAT), jnp.bfloat16),
            pltpu.VMEM((LEV, LAT), jnp.bfloat16),
            pltpu.VMEM((STEPS, LEV, LAT), jnp.bfloat16),
            pltpu.VMEM((LEV, LAT), jnp.float32),
            pltpu.VMEM((LON, LAT), jnp.float32),
            pltpu.VMEM((2, LON, LAT), jnp.float32),
            pltpu.VMEM((LON, LAT), jnp.int32),
            pltpu.VMEM((LON, LAT), jnp.int32),
            dma((4,)),
            dma((STEPS * PIECES, 3)),
            dma((STEPS * PIECES,)),
            dma((STEPS, 2, SLABS)),
            dma((STEPS, 2, SLABS)),
            dma((GROUP,)),
            dma((STEPS,)),
            dma((2,)),
            dma((2,)),
            dma((SLABS,)),
        ],
        compiler_params=pltpu.CompilerParams(
            collective_id=0, has_side_effects=True, vmem_limit_bytes=VMEM_LIMIT
        ),
    )(
        tracers.reshape(TRACERS, ROWS, LAT),
        archive.reshape(4, ROWS, LAT),
        sea_mask,
        levels,
    )
    return result.reshape(TRACERS, LEV, LON, LAT)


def solution(mesh):
    in_specs = (
        P("trc", None, "tile", None),
        P("trc", None, None, "tile", None),
        P("tile", None),
        P("tile", None),
    )
    return jax.shard_map(
        per_device, mesh=mesh, in_specs=in_specs, out_specs=P("trc", None, "tile", None), check_vma=False
    )
```

```python
import functools

import jax
import jax.numpy as jnp
from jax import lax
from jax.experimental import pallas as pl
from jax.experimental.pallas import tpu as pltpu
from jax.sharding import PartitionSpec as P

MESH = pl.DeviceIdType.MESH
STEPS = 3
DIFFUSION = 0.04
MIX_SCALE = 0.3
TRACERS, LEV, LON, LAT = 8, 48, 8, 256
HALF = LAT // 2
ROWS = LEV * LON
PAIRS = LEV // 2
TILES, GROUP = 32, 8

EVENTS = (
    (3, 1539, 3075, 1540, 3077, 1540, 6, 1542),
    (131, 1667, 3203, 1668, 3205, 3075, 134, 1670),
    (259, 1795, 3331, 1796, 3333, 1668, 262, 1798),
    (387, 1923, 3459, 1924, 3461, 3203, 390, 1926),
    (3076, 2051, 4, 1, 0, 1796, 1537, 1),
    (515, 2179, 3587, 2052, 3589, 3331, 3072, 2054),
    (3204, 2307, 132, 129, 128, 1924, 518, 129),
    (643, 3072, 3715, 2180, 3717, 3459, 1665, 2182),
    (3332, 2435, 260, 257, 256, 0, 3200, 257),
    (771, 3200, 3843, 2308, 3845, 2052, 646, 2310),
    (3460, 2563, 388, 385, 384, 3587, 1793, 385),
    (899, 3328, 1536, 3072, 1536, 128, 3328, 3072),
    (3588, 2691, 3971, 2436, 3973, 2180, 774, 2438),
    (1027, 3456, 516, 513, 512, 3715, 1921, 513),
    (3716, 2819, 1664, 3200, 1664, 256, 3456, 3200),
    (1155, 0, 4099, 2564, 4101, 2308, 902, 2566),
    (3844, 3584, 644, 641, 640, 3843, 2049, 641),
    (1283, 2947, 1792, 3328, 1792, 384, 3584, 3328),
    (1536, 128, 4227, 2692, 4229, 2436, 1030, 2694),
    (3972, 3712, 772, 769, 768, 3971, 2177, 769),
    (1411, 256, 1920, 3456, 1920, 512, 3712, 3456),
    (1664, 3840, 4355, 2820, 4357, 2564, 1158, 2822),
    (4100, 384, 900, 897, 896, 4099, 2305, 897),
    (1792, 3968, 2048, 3584, 2048, 640, 3840, 3584),
    (4228, 512, 4483, 2948, 4485, 2692, 1286, 2950),
    (1920, 4096, 1028, 1025, 1024, 4227, 2433, 1025),
    (4356, 640, 2176, 3712, 2176, 768, 3968, 3712),
    (2048, 4224, 1156, 1153, 1152, 2820, 1414, 1153),
    (4484, 768, 2304, 3840, 2304, 4355, 2561, 3840),
    (2176, 4352, 1284, 1281, 1280, 896, 4096, 1281),
    (2304, 896, 2432, 3968, 2432, 2948, 2689, 3968),
    (2432, 4480, 1412, 1409, 1408, 4483, 4224, 1409),
    (2560, 1024, 2560, 4096, 2560, 1024, 2817, 4096),
    (2688, 1152, 2688, 4224, 2688, 1152, 4352, 4224),
    (2816, 1280, 2816, 4352, 2816, 1280, 2945, 4352),
    (2944, 1408, 2944, 4480, 2944, 1408, 4480, 4480),
)
READY = ((19, 23, 27, 31, 34, 36), (22, 26, 30, 32, 34, 36), (15, 21, 27, 31, 34, 36))
SLABS = 6
AHEAD = 1
WAYS = ((1, 0), (3, 0), (0, 1), (2, 0), (1, 1), (3, 1), (2, 1))
PIECES = SLABS * 2
SLAB_ROWS = ROWS // SLABS
SLAB_PAIRS = PAIRS // SLABS
EARLY = 6
RELAY = 8
GROUPS = LEV // 8
RIM_ROWS = 8 * TRACERS
VMEM_LIMIT = 48 * 2**20


def batch(j):
    low = 0 if j == 0 else SLAB_PAIRS * j - 1
    high = PAIRS if j == SLABS - 1 else SLAB_PAIRS * (j + 1) - 1
    return low, high


def by_rank(rank, values):
    total = jnp.int32(values[0])
    for r in range(1, GROUP):
        if values[r] != values[0]:
            total = jnp.where(rank == r, jnp.int32(values[r]), total)
    return total


def kernel(
    tracers, archive, sea_mask_hbm, levels_hbm, out,
    cur_a, cur_b, rec, rim_out, rim_in, halo, zonal_f, masks, zonal_own, zrim_out, zrim_in, zrim, wet_out, wet_in, sea_mask, levels,
    load_sem, piece_send, piece_recv, rim_send, rim_recv, zrim_send, zrim_recv, wet_send, wet_recv, store_sem,
):
    tile = lax.axis_index("tile")
    rank = lax.axis_index("trc")
    x, z = rank // 2, rank % 2
    beside = [lax.rem(x + dx, 4) * 2 + lax.rem(z + dz, 2) for dx, dz in WAYS]
    east, west = lax.rem(tile + 1, TILES), lax.rem(tile + TILES - 1, TILES)

    first = [
        pltpu.make_async_copy(
            tracers.at[:, :, pl.ds(HALF * h, HALF)], cur_a.at[h, :, pl.ds(8, ROWS)], load_sem.at[(0, 4)[h]]
        )
        for h in range(2)
    ]
    own = pltpu.make_async_copy(archive.at[0], zonal_own, load_sem.at[1])

    def piece_ref(ref, record, half, slab):
        rows = pl.ds(pl.multiple_of(slab * SLAB_ROWS, SLAB_ROWS), SLAB_ROWS)
        if record is None:
            return ref.at[pl.ds(2 * half, 2), rows]
        return ref.at[record, pl.ds(2 * half, 2), rows]

    for r in range(STEPS):
        @pl.when(rank == r)
        def _():
            for j in range(SLABS):
                for h in range(2):
                    pltpu.make_async_copy(
                        piece_ref(archive, None, h, j), piece_ref(rec, r, h, j), piece_recv.at[r * PIECES + 2 * j + h]
                    ).start()

    @pl.when(rank < STEPS)
    def _():
        own.start()

    maps = [
        pltpu.make_async_copy(src, dst, load_sem.at[2 + i])
        for i, (src, dst) in enumerate(((sea_mask_hbm, sea_mask), (levels_hbm, levels)))
    ]
    for c in maps:
        c.start()
    for c in first:
        c.start()

    barrier = pltpu.get_barrier_semaphore()
    for k in range(1, GROUP):
        pl.semaphore_signal(barrier, inc=1, device_id={"trc": lax.rem(rank + k, GROUP)}, device_id_type=MESH)
    for n in (east, west):
        pl.semaphore_signal(barrier, inc=1, device_id={"tile": n}, device_id_type=MESH)

    row = lax.broadcasted_iota(jnp.int32, (2, LON, LAT), 1)
    lane = lax.broadcasted_iota(jnp.int32, (LON, LAT), 1)
    level_of = lax.broadcasted_iota(jnp.int32, (3, LON, LAT), 0)
    row_a = row[0]

    for c in maps:
        c.wait()
    depth = sea_mask[...] * levels[...]
    wet_out[...] = depth.astype(jnp.float32)
    for ref in (cur_a, cur_b):
        for h in range(2):
            for t in range(TRACERS):
                ref[h, t, pl.ds(0, 8)] = jnp.zeros((8, HALF), jnp.float32)
                ref[h, t, pl.ds(ROWS + 8, 8)] = jnp.zeros((8, HALF), jnp.float32)
    pl.semaphore_wait(barrier, GROUP + 1)

    def tile_copy(src, dst, send, recv, to):
        return pltpu.make_async_remote_copy(
            src_ref=src, dst_ref=dst, send_sem=send, recv_sem=recv, device_id={"tile": to}, device_id_type=MESH
        )

    wet_copies = [
        tile_copy(wet_out, wet_in.at[side], wet_send.at[side], wet_recv.at[side], to)
        for side, to in ((0, east), (1, west))
    ]
    for c in wet_copies:
        c.start()

    words = []
    for e in range(0, len(EVENTS), 2):
        words.append(by_rank(rank, [EVENTS[e][r] + (EVENTS[e + 1][r] << 14) for r in range(GROUP)]))

    def event_parts(e):
        code = words[e // 2] % (1 << 14) if e % 2 == 0 else words[e // 2] // (1 << 14)
        return code // 128, code % 128

    def hand_on(p, d):
        ref = piece_ref(rec, p // PIECES, p % 2, (p % PIECES) // 2)
        return pltpu.make_async_remote_copy(
            src_ref=ref, dst_ref=ref, send_sem=piece_send.at[p, d], recv_sem=piece_recv.at[p],
            device_id={"trc": beside[d]}, device_id_type=MESH,
        )

    def event(e):
        p, dirs = event_parts(e)
        ref = piece_ref(rec, p // PIECES, p % 2, (p % PIECES) // 2)
        pltpu.make_async_copy(ref, ref, piece_recv.at[p]).wait()
        for d in range(len(WAYS)):
            if any((v >> d) & 1 for v in EVENTS[e]):
                @pl.when((dirs // (1 << d)) % 2 == 1)
                def _():
                    hand_on(p, d).start()

    def rim_copies(s, g):
        rows = pl.ds(RIM_ROWS * g, RIM_ROWS)
        return [
            tile_copy(
                rim_out.at[s, side, rows], rim_in.at[s, side, rows], rim_send.at[s, side, g], rim_recv.at[s, side, g], to
            )
            for side, to in ((0, east), (1, west))
        ]

    def send_rims(s, g, ref):
        for side, lon in ((0, LON - 1), (1, 0)):
            for t in range(0, TRACERS, 2):
                for h in range(2):
                    both = [ref[h, t + k, pl.ds(8 + 64 * g + lon, 8, stride=LON)] for k in range(2)]
                    both = jnp.concatenate(both, axis=0).astype(jnp.bfloat16)
                    rim_out[s, side, pl.ds(RIM_ROWS * g + 8 * t, 16), HALF * h : HALF * (h + 1)] = both
        for c in rim_copies(s, g):
            c.start()

    def early_events():
        for e in range(EARLY):
            event(e)

    @pl.when(rank == 0)
    def _():
        early_events()

    def zrim_west(r):
        return tile_copy(zrim_out, zrim_in.at[r], zrim_send.at[0], zrim_recv.at[r], west)

    def zrim_round(r, k):
        return pltpu.make_async_remote_copy(
            src_ref=zrim_in.at[r], dst_ref=zrim_in.at[r], send_sem=zrim_send.at[k], recv_sem=zrim_recv.at[r],
            device_id={"trc": lax.rem(rank + k, GROUP)}, device_id_type=MESH,
        )

    @pl.when(rank < STEPS)
    def _():
        own.wait()
        for h in range(2):
            cols = slice(HALF * h, HALF * (h + 1))
            zonal_f[h] = zonal_own[:, cols].astype(jnp.float32)
            for g in range(LEV // 16):
                value = [zonal_f[h, pl.ds(128 * g + 64 * k, 8, stride=LON)] for k in range(2)]
                zrim_out[pl.ds(16 * g, 16), cols] = jnp.concatenate(value, axis=0).astype(jnp.bfloat16)

    for r in range(STEPS):
        @pl.when(rank == r)
        def _():
            zrim_west(r).start()

    for c in first:
        c.wait()
    for g in range(GROUPS):
        send_rims(0, g, cur_a)

    @pl.when(rank != 0)
    def _():
        early_events()

    def zrims_round():
        for r in range(STEPS):
            @pl.when(rank == r)
            def _():
                zrim_west(r).wait_recv()
                for k in range(1, GROUP):
                    zrim_round(r, k).start()

    def make_masks():
        for c in wet_copies:
            c.wait()
        depth_w, depth_e = wet_in[0, 7:8], wet_in[1, 0:1]
        depth_f = depth.astype(jnp.float32)
        beyond_w = jnp.where(row_a == 0, depth_w, pltpu.roll(depth_f, 1, 0))
        beyond_e = jnp.where(row_a == LON - 1, depth_e, pltpu.roll(depth_f, LON - 1, 0))
        beyond_s = jnp.where(lane == 0, 0.0, pltpu.roll(depth_f, 1, 1))
        beyond_n = jnp.where(lane == LAT - 1, 0.0, pltpu.roll(depth_f, LAT - 1, 1))
        for i, beyond in enumerate((beyond_w, beyond_e, beyond_s, beyond_n)):
            masks[i] = jnp.minimum(depth_f, beyond)
        masks[4] = depth_f

    def work(s, j, source, target):
        low, high = batch(j)
        before = 0 if j == 0 else (2 * low - 1) // 8 + 1
        for g in range(before, (2 * high - 1) // 8 + 1):
            for c in rim_copies(s, g):
                c.wait_recv()
            for side in range(2):
                rows = pl.ds(RIM_ROWS * g, RIM_ROWS)
                halo[side, rows] = rim_in[s, side, rows].astype(jnp.float32)

        def pair(p, _):
            start = pl.multiple_of(16 * p, 16)
            after = pl.multiple_of(16 * p + 16, 16)
            level3 = (level_of + 2 * p).astype(jnp.float32)
            level2 = level3[:2]

            def field(f, at):
                return rec[s, f, pl.ds(at, 16)].astype(jnp.float32).reshape(2, LON, LAT)

            def two_sided(courant, mask):
                plus = jnp.maximum(courant, 0.0) + DIFFUSION
                wet = mask[None] > level2
                return jnp.where(wet, plus, 0.0), jnp.where(wet, plus - courant, 0.0)

            zonal = field(0, start)
            zonal_e = pltpu.roll(zonal, LON - 1, 1)
            rims = [jnp.broadcast_to(zrim[pl.ds(2 * p + k, 1)], (LON, LAT)) for k in range(2)]
            zonal_e = jnp.where(row == LON - 1, jnp.stack(rims), zonal_e)
            from_w, to_w = two_sided(zonal, masks[0])
            to_e, from_e = two_sided(zonal_e, masks[1])
            merid = field(1, start)
            from_s, to_s = two_sided(merid, masks[2])
            to_n, from_n = two_sided(pltpu.roll(merid, LAT - 1, 2), masks[3])
            upward = jnp.concatenate([field(2, start), field(2, after)[:1]], axis=0)
            mixing = MIX_SCALE * jnp.abs(jnp.concatenate([field(3, start), field(3, after)[:1]], axis=0))
            wet3 = jnp.logical_and(masks[4][None] > level3, level3 > 0.0)
            plus3 = jnp.maximum(upward, 0.0) + mixing
            lower = jnp.where(wet3, plus3, 0.0)
            upper = jnp.where(wet3, plus3 - upward, 0.0)
            from_below, to_above = lower[1:], lower[:2]
            from_above, to_below = upper[:2], upper[1:]
            stay = 1.0 - (to_w + to_e + to_s + to_n + to_above + to_below)

            at = (p // 4) * RIM_ROWS + (p % 4) * 2
            for t in range(TRACERS):
                four = jnp.concatenate([source[h, t, pl.ds(start, 32)] for h in range(2)], axis=1).reshape(4, LON, LAT)
                here = four[1:3]
                side_w = jnp.stack([jnp.broadcast_to(halo[0, pl.ds(at + (8 * t + k), 1)], (LON, LAT)) for k in range(2)])
                side_e = jnp.stack([jnp.broadcast_to(halo[1, pl.ds(at + (8 * t + k), 1)], (LON, LAT)) for k in range(2)])
                at_w = jnp.where(row == 0, side_w, pltpu.roll(here, 1, 1))
                at_e = jnp.where(row == LON - 1, side_e, pltpu.roll(here, LON - 1, 1))
                new = stay * here + from_w * at_w + from_e * at_e
                new += from_s * pltpu.roll(here, 1, 2) + from_n * pltpu.roll(here, LAT - 1, 2)
                new += from_below * four[2:4] + from_above * four[0:2]
                new = new.reshape(16, LAT)
                for h in range(2):
                    target[h, t, pl.ds(pl.multiple_of(start + 8, 8), 16)] = new[:, HALF * h : HALF * (h + 1)]
            return 0

        lax.fori_loop(low, high, pair, 0)
        if s < STEPS - 1:
            for g in range(2 * low // 8, 2 * high // 8):
                send_rims(s + 1, g, target)

    done = EARLY
    stores = []
    for s in range(STEPS):
        source, target = ((cur_a, cur_b), (cur_b, cur_a))[s % 2]
        for j in range(SLABS):
            upto = READY[s][j]
            if s < STEPS - 1 or j < SLABS - 1:
                upto = min(len(EVENTS), upto + AHEAD)
            for e in range(done, upto):
                if e == RELAY:
                    zrims_round()
                event(e)
            done = max(done, upto)
            if j == 0 and s == 0:
                make_masks()
            if j == 0:
                @pl.when(rank != s)
                def _():
                    zrim_west(s).wait_recv()
                zrim[...] = zrim_in[s].astype(jnp.float32)
            work(s, j, source, target)
            if s == STEPS - 1:
                low, high = batch(j)
                count = 16 * (high - low)
                for h in range(2):
                    c = pltpu.make_async_copy(
                        target.at[h, :, pl.ds(8 + 16 * low, count)],
                        out.at[:, pl.ds(16 * low, count), pl.ds(HALF * h, HALF)],
                        store_sem.at[j, h],
                    )
                    c.start()
                    stores.append(c)

    for s in range(STEPS):
        for g in range(GROUPS):
            for c in rim_copies(s, g):
                c.wait_send()
    for r in range(STEPS):
        @pl.when(rank == r)
        def _():
            zrim_west(r).wait_send()
            for k in range(1, GROUP):
                zrim_round(r, k).wait_send()
    for e in range(len(EVENTS)):
        p, dirs = event_parts(e)
        for d in range(len(WAYS)):
            if any((v >> d) & 1 for v in EVENTS[e]):
                @pl.when((dirs // (1 << d)) % 2 == 1)
                def _():
                    hand_on(p, d).wait_send()
    for c in stores:
        c.wait()


def per_device(tracers, archive, sea_mask, levels):
    any_space = pl.BlockSpec(memory_space=pl.ANY)
    in_hbm = pl.BlockSpec(memory_space=pltpu.HBM)
    dma = pltpu.SemaphoreType.DMA
    result = pl.pallas_call(
        kernel,
        out_shape=jax.ShapeDtypeStruct((TRACERS, ROWS, LAT), jnp.float32),
        in_specs=[in_hbm, in_hbm, in_hbm, in_hbm],
        out_specs=any_space,
        scratch_shapes=[
            pltpu.VMEM((2, TRACERS, ROWS + 16, HALF), jnp.float32),
            pltpu.VMEM((2, TRACERS, ROWS + 16, HALF), jnp.float32),
            pltpu.VMEM((STEPS, 4, ROWS + 16, LAT), jnp.bfloat16),
            pltpu.VMEM((STEPS, 2, ROWS, LAT), jnp.bfloat16),
            pltpu.VMEM((STEPS, 2, ROWS, LAT), jnp.bfloat16),
            pltpu.VMEM((2, ROWS, LAT), jnp.float32),
            pltpu.VMEM((2, ROWS, HALF), jnp.float32),
            pltpu.VMEM((5, LON, LAT), jnp.float32),
            pltpu.VMEM((ROWS, LAT), jnp.bfloat16),
            pltpu.VMEM((LEV, LAT), jnp.bfloat16),
            pltpu.VMEM((STEPS, LEV, LAT), jnp.bfloat16),
            pltpu.VMEM((LEV, LAT), jnp.float32),
            pltpu.VMEM((LON, LAT), jnp.float32),
            pltpu.VMEM((2, LON, LAT), jnp.float32),
            pltpu.VMEM((LON, LAT), jnp.int32),
            pltpu.VMEM((LON, LAT), jnp.int32),
            dma((5,)),
            dma((STEPS * PIECES, len(WAYS))),
            dma((STEPS * PIECES,)),
            dma((STEPS, 2, GROUPS)),
            dma((STEPS, 2, GROUPS)),
            dma((GROUP,)),
            dma((STEPS,)),
            dma((2,)),
            dma((2,)),
            dma((SLABS, 2)),
        ],
        compiler_params=pltpu.CompilerParams(
            collective_id=0, has_side_effects=True, vmem_limit_bytes=VMEM_LIMIT
        ),
    )(
        tracers.reshape(TRACERS, ROWS, LAT),
        archive.reshape(4, ROWS, LAT),
        sea_mask,
        levels,
    )
    return result.reshape(TRACERS, LEV, LON, LAT)


def solution(mesh):
    in_specs = (
        P("trc", None, "tile", None),
        P("trc", None, None, "tile", None),
        P("tile", None),
        P("tile", None),
    )
    return jax.shard_map(
        per_device, mesh=mesh, in_specs=in_specs, out_specs=P("trc", None, "tile", None), check_vma=False
    )
```

```python
import functools

import jax
import jax.numpy as jnp
from jax import lax
from jax.experimental import pallas as pl
from jax.experimental.pallas import tpu as pltpu
from jax.sharding import PartitionSpec as P

MESH = pl.DeviceIdType.MESH
STEPS = 3
DIFFUSION = 0.04
MIX_SCALE = 0.3
TRACERS, LEV, LON, LAT = 8, 48, 8, 256
HALF = LAT // 2
ROWS = LEV * LON
PAIRS = LEV // 2
TILES, GROUP = 32, 8

EVENTS = (
    (3, 1539, 3075, 1540, 3077, 1540, 6, 1542),
    (131, 1667, 3203, 1668, 3205, 3075, 134, 1670),
    (259, 1795, 3331, 1796, 3333, 1668, 262, 1798),
    (387, 1923, 3459, 1924, 3461, 3203, 390, 1926),
    (3076, 2051, 4, 1, 0, 1796, 1537, 1),
    (515, 2179, 3587, 2052, 3589, 3331, 3072, 2054),
    (3204, 2307, 132, 129, 128, 1924, 518, 129),
    (643, 3072, 3715, 2180, 3717, 3459, 1665, 2182),
    (3332, 2435, 260, 257, 256, 0, 3200, 257),
    (771, 3200, 3843, 2308, 3845, 2052, 646, 2310),
    (3460, 2563, 388, 385, 384, 3587, 1793, 385),
    (899, 3328, 1536, 3072, 1536, 128, 3328, 3072),
    (3588, 2691, 3971, 2436, 3973, 2180, 774, 2438),
    (1027, 3456, 516, 513, 512, 3715, 1921, 513),
    (3716, 2819, 1664, 3200, 1664, 256, 3456, 3200),
    (1155, 0, 4099, 2564, 4101, 2308, 902, 2566),
    (3844, 3584, 644, 641, 640, 3843, 2049, 641),
    (1283, 2947, 1792, 3328, 1792, 384, 3584, 3328),
    (1536, 128, 4227, 2692, 4229, 2436, 1030, 2694),
    (3972, 3712, 772, 769, 768, 3971, 2177, 769),
    (1411, 256, 1920, 3456, 1920, 512, 3712, 3456),
    (1664, 3840, 4355, 2820, 4357, 2564, 1158, 2822),
    (4100, 384, 900, 897, 896, 4099, 2305, 897),
    (1792, 3968, 2048, 3584, 2048, 640, 3840, 3584),
    (4228, 512, 4483, 2948, 4485, 2692, 1286, 2950),
    (1920, 4096, 1028, 1025, 1024, 4227, 2433, 1025),
    (4356, 640, 2176, 3712, 2176, 768, 3968, 3712),
    (2048, 4224, 1156, 1153, 1152, 2820, 1414, 1153),
    (4484, 768, 2304, 3840, 2304, 4355, 2561, 3840),
    (2176, 4352, 1284, 1281, 1280, 896, 4096, 1281),
    (2304, 896, 2432, 3968, 2432, 2948, 2689, 3968),
    (2432, 4480, 1412, 1409, 1408, 4483, 4224, 1409),
    (2560, 1024, 2560, 4096, 2560, 1024, 2817, 4096),
    (2688, 1152, 2688, 4224, 2688, 1152, 4352, 4224),
    (2816, 1280, 2816, 4352, 2816, 1280, 2945, 4352),
    (2944, 1408, 2944, 4480, 2944, 1408, 4480, 4480),
)
READY = ((16, 19, 21, 23, 25, 27, 29, 31, 33, 34, 35, 36), (19, 22, 24, 26, 28, 30, 31, 32, 33, 34, 35, 36), (12, 15, 18, 21, 24, 27, 29, 31, 33, 34, 35, 36))
SLABS = 12
AHEAD = 0
WAYS = ((1, 0), (3, 0), (0, 1), (2, 0), (1, 1), (3, 1), (2, 1))
PIECES = SLABS
SLAB_ROWS = ROWS // SLABS
SLAB_PAIRS = PAIRS // SLABS
EARLY = 6
RELAY = 8
GROUPS = LEV // 8
RIM_ROWS = 8 * TRACERS
VMEM_LIMIT = 48 * 2**20


def batch(j):
    low = 0 if j == 0 else SLAB_PAIRS * j - 1
    high = PAIRS if j == SLABS - 1 else SLAB_PAIRS * (j + 1) - 1
    return low, high


def by_rank(rank, values):
    total = jnp.int32(values[0])
    for r in range(1, GROUP):
        if values[r] != values[0]:
            total = jnp.where(rank == r, jnp.int32(values[r]), total)
    return total


def kernel(
    tracers, archive, sea_mask_hbm, levels_hbm, out,
    cur_a, cur_b, rec, rim_out, rim_in, halo, zonal_f, masks, zonal_own, zrim_out, zrim_in, zrim, wet_out, wet_in, sea_mask, levels,
    load_sem, piece_send, piece_recv, rim_send, rim_recv, zrim_send, zrim_recv, wet_send, wet_recv, store_sem,
):
    tile = lax.axis_index("tile")
    rank = lax.axis_index("trc")
    x, z = rank // 2, rank % 2
    beside = [lax.rem(x + dx, 4) * 2 + lax.rem(z + dz, 2) for dx, dz in WAYS]
    east, west = lax.rem(tile + 1, TILES), lax.rem(tile + TILES - 1, TILES)

    first = [
        pltpu.make_async_copy(
            tracers.at[:, :, pl.ds(HALF * h, HALF)], cur_a.at[h, :, pl.ds(8, ROWS)], load_sem.at[(0, 4)[h]]
        )
        for h in range(2)
    ]
    own = pltpu.make_async_copy(archive.at[0], zonal_own, load_sem.at[1])

    def piece_ref(ref, record, slab):
        rows = pl.ds(pl.multiple_of(slab * SLAB_ROWS, SLAB_ROWS), SLAB_ROWS)
        if record is None:
            return ref.at[:, rows]
        return ref.at[record, :, rows]

    for r in range(STEPS):
        @pl.when(rank == r)
        def _():
            for j in range(SLABS):
                pltpu.make_async_copy(
                    piece_ref(archive, None, j), piece_ref(rec, r, j), piece_recv.at[r * PIECES + j]
                ).start()

    @pl.when(rank < STEPS)
    def _():
        own.start()

    maps = [
        pltpu.make_async_copy(src, dst, load_sem.at[2 + i])
        for i, (src, dst) in enumerate(((sea_mask_hbm, sea_mask), (levels_hbm, levels)))
    ]
    for c in maps:
        c.start()
    for c in first:
        c.start()

    barrier = pltpu.get_barrier_semaphore()
    for k in range(1, GROUP):
        pl.semaphore_signal(barrier, inc=1, device_id={"trc": lax.rem(rank + k, GROUP)}, device_id_type=MESH)
    for n in (east, west):
        pl.semaphore_signal(barrier, inc=1, device_id={"tile": n}, device_id_type=MESH)

    row = lax.broadcasted_iota(jnp.int32, (2, LON, LAT), 1)
    lane = lax.broadcasted_iota(jnp.int32, (LON, LAT), 1)
    level_of = lax.broadcasted_iota(jnp.int32, (3, LON, LAT), 0)
    row_a = row[0]

    for c in maps:
        c.wait()
    depth = sea_mask[...] * levels[...]
    wet_out[...] = depth.astype(jnp.float32)
    for ref in (cur_a, cur_b):
        for h in range(2):
            for t in range(TRACERS):
                ref[h, t, pl.ds(0, 8)] = jnp.zeros((8, HALF), jnp.float32)
                ref[h, t, pl.ds(ROWS + 8, 8)] = jnp.zeros((8, HALF), jnp.float32)
    pl.semaphore_wait(barrier, GROUP + 1)

    def tile_copy(src, dst, send, recv, to):
        return pltpu.make_async_remote_copy(
            src_ref=src, dst_ref=dst, send_sem=send, recv_sem=recv, device_id={"tile": to}, device_id_type=MESH
        )

    wet_copies = [
        tile_copy(wet_out, wet_in.at[side], wet_send.at[side], wet_recv.at[side], to)
        for side, to in ((0, east), (1, west))
    ]
    for c in wet_copies:
        c.start()

    words = []
    for e in range(0, len(EVENTS), 2):
        words.append(by_rank(rank, [EVENTS[e][r] + (EVENTS[e + 1][r] << 14) for r in range(GROUP)]))

    def event_parts(e):
        code = words[e // 2] % (1 << 14) if e % 2 == 0 else words[e // 2] // (1 << 14)
        return code // 128, code % 128

    def hand_on(p, d):
        ref = piece_ref(rec, p // PIECES, p % PIECES)
        return pltpu.make_async_remote_copy(
            src_ref=ref, dst_ref=ref, send_sem=piece_send.at[p, d], recv_sem=piece_recv.at[p],
            device_id={"trc": beside[d]}, device_id_type=MESH,
        )

    def event(e):
        p, dirs = event_parts(e)
        ref = piece_ref(rec, p // PIECES, p % PIECES)
        pltpu.make_async_copy(ref, ref, piece_recv.at[p]).wait()
        for d in range(len(WAYS)):
            if any((v >> d) & 1 for v in EVENTS[e]):
                @pl.when((dirs // (1 << d)) % 2 == 1)
                def _():
                    hand_on(p, d).start()

    def rim_copies(s, g):
        rows = pl.ds(RIM_ROWS * g, RIM_ROWS)
        return [
            tile_copy(
                rim_out.at[s, side, rows], rim_in.at[s, side, rows], rim_send.at[s, side, g], rim_recv.at[s, side, g], to
            )
            for side, to in ((0, east), (1, west))
        ]

    def send_rims(s, g, ref):
        for side, lon in ((0, LON - 1), (1, 0)):
            for t in range(0, TRACERS, 2):
                for h in range(2):
                    both = [ref[h, t + k, pl.ds(8 + 64 * g + lon, 8, stride=LON)] for k in range(2)]
                    both = jnp.concatenate(both, axis=0).astype(jnp.bfloat16)
                    rim_out[s, side, pl.ds(RIM_ROWS * g + 8 * t, 16), HALF * h : HALF * (h + 1)] = both
        for c in rim_copies(s, g):
            c.start()

    def early_events():
        for e in range(EARLY):
            event(e)

    @pl.when(rank == 0)
    def _():
        early_events()

    def zrim_west(r):
        return tile_copy(zrim_out, zrim_in.at[r], zrim_send.at[0], zrim_recv.at[r], west)

    def zrim_round(r, k):
        return pltpu.make_async_remote_copy(
            src_ref=zrim_in.at[r], dst_ref=zrim_in.at[r], send_sem=zrim_send.at[k], recv_sem=zrim_recv.at[r],
            device_id={"trc": lax.rem(rank + k, GROUP)}, device_id_type=MESH,
        )

    @pl.when(rank < STEPS)
    def _():
        own.wait()
        for h in range(2):
            cols = slice(HALF * h, HALF * (h + 1))
            zonal_f[h] = zonal_own[:, cols].astype(jnp.float32)
            for g in range(LEV // 16):
                value = [zonal_f[h, pl.ds(128 * g + 64 * k, 8, stride=LON)] for k in range(2)]
                zrim_out[pl.ds(16 * g, 16), cols] = jnp.concatenate(value, axis=0).astype(jnp.bfloat16)

    for r in range(STEPS):
        @pl.when(rank == r)
        def _():
            zrim_west(r).start()

    for c in first:
        c.wait()
    for g in range(GROUPS):
        send_rims(0, g, cur_a)

    @pl.when(rank != 0)
    def _():
        early_events()

    def zrims_round():
        for r in range(STEPS):
            @pl.when(rank == r)
            def _():
                zrim_west(r).wait_recv()
                for k in range(1, GROUP):
                    zrim_round(r, k).start()

    def make_masks():
        for c in wet_copies:
            c.wait()
        depth_w, depth_e = wet_in[0, 7:8], wet_in[1, 0:1]
        depth_f = depth.astype(jnp.float32)
        beyond_w = jnp.where(row_a == 0, depth_w, pltpu.roll(depth_f, 1, 0))
        beyond_e = jnp.where(row_a == LON - 1, depth_e, pltpu.roll(depth_f, LON - 1, 0))
        beyond_s = jnp.where(lane == 0, 0.0, pltpu.roll(depth_f, 1, 1))
        beyond_n = jnp.where(lane == LAT - 1, 0.0, pltpu.roll(depth_f, LAT - 1, 1))
        for i, beyond in enumerate((beyond_w, beyond_e, beyond_s, beyond_n)):
            masks[i] = jnp.minimum(depth_f, beyond)
        masks[4] = depth_f

    def work(s, j, source, target):
        low, high = batch(j)
        before = 0 if j == 0 else (2 * low - 1) // 8 + 1
        for g in range(before, (2 * high - 1) // 8 + 1):
            for c in rim_copies(s, g):
                c.wait_recv()
            for side in range(2):
                rows = pl.ds(RIM_ROWS * g, RIM_ROWS)
                halo[side, rows] = rim_in[s, side, rows].astype(jnp.float32)

        def pair(p, _):
            start = pl.multiple_of(16 * p, 16)
            after = pl.multiple_of(16 * p + 16, 16)
            level3 = (level_of + 2 * p).astype(jnp.float32)
            level2 = level3[:2]

            def field(f, at):
                return rec[s, f, pl.ds(at, 16)].astype(jnp.float32).reshape(2, LON, LAT)

            def two_sided(courant, mask):
                plus = jnp.maximum(courant, 0.0) + DIFFUSION
                wet = mask[None] > level2
                return jnp.where(wet, plus, 0.0), jnp.where(wet, plus - courant, 0.0)

            zonal = field(0, start)
            zonal_e = pltpu.roll(zonal, LON - 1, 1)
            rims = [jnp.broadcast_to(zrim[pl.ds(2 * p + k, 1)], (LON, LAT)) for k in range(2)]
            zonal_e = jnp.where(row == LON - 1, jnp.stack(rims), zonal_e)
            from_w, to_w = two_sided(zonal, masks[0])
            to_e, from_e = two_sided(zonal_e, masks[1])
            merid = field(1, start)
            from_s, to_s = two_sided(merid, masks[2])
            to_n, from_n = two_sided(pltpu.roll(merid, LAT - 1, 2), masks[3])
            upward = jnp.concatenate([field(2, start), field(2, after)[:1]], axis=0)
            mixing = MIX_SCALE * jnp.abs(jnp.concatenate([field(3, start), field(3, after)[:1]], axis=0))
            wet3 = jnp.logical_and(masks[4][None] > level3, level3 > 0.0)
            plus3 = jnp.maximum(upward, 0.0) + mixing
            lower = jnp.where(wet3, plus3, 0.0)
            upper = jnp.where(wet3, plus3 - upward, 0.0)
            from_below, to_above = lower[1:], lower[:2]
            from_above, to_below = upper[:2], upper[1:]
            stay = 1.0 - (to_w + to_e + to_s + to_n + to_above + to_below)

            at = (p // 4) * RIM_ROWS + (p % 4) * 2
            for t in range(TRACERS):
                four = jnp.concatenate([source[h, t, pl.ds(start, 32)] for h in range(2)], axis=1).reshape(4, LON, LAT)
                here = four[1:3]
                side_w = jnp.stack([jnp.broadcast_to(halo[0, pl.ds(at + (8 * t + k), 1)], (LON, LAT)) for k in range(2)])
                side_e = jnp.stack([jnp.broadcast_to(halo[1, pl.ds(at + (8 * t + k), 1)], (LON, LAT)) for k in range(2)])
                at_w = jnp.where(row == 0, side_w, pltpu.roll(here, 1, 1))
                at_e = jnp.where(row == LON - 1, side_e, pltpu.roll(here, LON - 1, 1))
                new = stay * here + from_w * at_w + from_e * at_e
                new += from_s * pltpu.roll(here, 1, 2) + from_n * pltpu.roll(here, LAT - 1, 2)
                new += from_below * four[2:4] + from_above * four[0:2]
                new = new.reshape(16, LAT)
                for h in range(2):
                    target[h, t, pl.ds(pl.multiple_of(start + 8, 8), 16)] = new[:, HALF * h : HALF * (h + 1)]
            return 0

        lax.fori_loop(low, high, pair, 0)
        if s < STEPS - 1:
            for g in range(2 * low // 8, 2 * high // 8):
                send_rims(s + 1, g, target)

    done = EARLY
    stores = []
    for s in range(STEPS):
        source, target = ((cur_a, cur_b), (cur_b, cur_a))[s % 2]
        for j in range(SLABS):
            upto = READY[s][j]
            if s < STEPS - 1 or j < SLABS - 1:
                upto = min(len(EVENTS), upto + AHEAD)
            for e in range(done, upto):
                if e == RELAY:
                    zrims_round()
                event(e)
            done = max(done, upto)
            if j == 0 and s == 0:
                make_masks()
            if j == 0:
                @pl.when(rank != s)
                def _():
                    zrim_west(s).wait_recv()
                zrim[...] = zrim_in[s].astype(jnp.float32)
            work(s, j, source, target)
            if s == STEPS - 1:
                low, high = batch(j)
                count = 16 * (high - low)
                for h in range(2):
                    c = pltpu.make_async_copy(
                        target.at[h, :, pl.ds(8 + 16 * low, count)],
                        out.at[:, pl.ds(16 * low, count), pl.ds(HALF * h, HALF)],
                        store_sem.at[j, h],
                    )
                    c.start()
                    stores.append(c)

    for s in range(STEPS):
        for g in range(GROUPS):
            for c in rim_copies(s, g):
                c.wait_send()
    for r in range(STEPS):
        @pl.when(rank == r)
        def _():
            zrim_west(r).wait_send()
            for k in range(1, GROUP):
                zrim_round(r, k).wait_send()
    for e in range(len(EVENTS)):
        p, dirs = event_parts(e)
        for d in range(len(WAYS)):
            if any((v >> d) & 1 for v in EVENTS[e]):
                @pl.when((dirs // (1 << d)) % 2 == 1)
                def _():
                    hand_on(p, d).wait_send()
    for c in stores:
        c.wait()


def per_device(tracers, archive, sea_mask, levels):
    any_space = pl.BlockSpec(memory_space=pl.ANY)
    in_hbm = pl.BlockSpec(memory_space=pltpu.HBM)
    dma = pltpu.SemaphoreType.DMA
    result = pl.pallas_call(
        kernel,
        out_shape=jax.ShapeDtypeStruct((TRACERS, ROWS, LAT), jnp.float32),
        in_specs=[in_hbm, in_hbm, in_hbm, in_hbm],
        out_specs=any_space,
        scratch_shapes=[
            pltpu.VMEM((2, TRACERS, ROWS + 16, HALF), jnp.float32),
            pltpu.VMEM((2, TRACERS, ROWS + 16, HALF), jnp.float32),
            pltpu.VMEM((STEPS, 4, ROWS + 16, LAT), jnp.bfloat16),
            pltpu.VMEM((STEPS, 2, ROWS, LAT), jnp.bfloat16),
            pltpu.VMEM((STEPS, 2, ROWS, LAT), jnp.bfloat16),
            pltpu.VMEM((2, ROWS, LAT), jnp.float32),
            pltpu.VMEM((2, ROWS, HALF), jnp.float32),
            pltpu.VMEM((5, LON, LAT), jnp.float32),
            pltpu.VMEM((ROWS, LAT), jnp.bfloat16),
            pltpu.VMEM((LEV, LAT), jnp.bfloat16),
            pltpu.VMEM((STEPS, LEV, LAT), jnp.bfloat16),
            pltpu.VMEM((LEV, LAT), jnp.float32),
            pltpu.VMEM((LON, LAT), jnp.float32),
            pltpu.VMEM((2, LON, LAT), jnp.float32),
            pltpu.VMEM((LON, LAT), jnp.int32),
            pltpu.VMEM((LON, LAT), jnp.int32),
            dma((5,)),
            dma((STEPS * PIECES, len(WAYS))),
            dma((STEPS * PIECES,)),
            dma((STEPS, 2, GROUPS)),
            dma((STEPS, 2, GROUPS)),
            dma((GROUP,)),
            dma((STEPS,)),
            dma((2,)),
            dma((2,)),
            dma((SLABS, 2)),
        ],
        compiler_params=pltpu.CompilerParams(
            collective_id=0, has_side_effects=True, vmem_limit_bytes=VMEM_LIMIT
        ),
    )(
        tracers.reshape(TRACERS, ROWS, LAT),
        archive.reshape(4, ROWS, LAT),
        sea_mask,
        levels,
    )
    return result.reshape(TRACERS, LEV, LON, LAT)


def solution(mesh):
    in_specs = (
        P("trc", None, "tile", None),
        P("trc", None, None, "tile", None),
        P("tile", None),
        P("tile", None),
    )
    return jax.shard_map(
        per_device, mesh=mesh, in_specs=in_specs, out_specs=P("trc", None, "tile", None), check_vma=False
    )
```
